32 devices in a mesh: groups: 2 (over x), leaf: 16 (over z, y, core).
Axes of the slice: x: 2, y: 2, z: 4, core: 2. Of those that a mesh axis runs over, the one named last changes fastest.
Arguments:
- vectors: bfloat16 [8, 65536], P(None, ('groups', 'leaf')), parts along dimension 1, may hold values from -6 to 6
- leaf_bases: bfloat16 [1024, 4096], P(('groups', 'leaf')), parts along dimension 0, may hold values from -0.75 to 0.75
- transfer_low: bfloat16 [1024, 4096], P(('groups', 'leaf')), parts along dimension 0, may hold values from -0.75 to 0.75
- transfer_mid: bfloat16 [512, 4096], P(('groups', 'leaf')), parts along dimension 0, may hold values from -0.75 to 0.75
- leaf_coupling_matrices: bfloat16 [1024, 4, 4096], P(('groups', 'leaf')), parts along dimension 0, may hold values from -0.375 to 0.375
- coupling_mid: bfloat16 [512, 8, 4096], P(('groups', 'leaf')), parts along dimension 0, may hold values from -0.25 to 0.25
- coupling_top: bfloat16 [256, 16, 4096], P(('groups', 'leaf')), parts along dimension 0, may hold values from -0.1875 to 0.1875
- near_blocks: bfloat16 [1024, 4, 4096], P(('groups', 'leaf')), parts along dimension 0, may hold values from -0.375 to 0.375
- partners_leaf: int32 [1024, 4], P(('groups', 'leaf')), parts along dimension 0, may hold values from 0 to 511, as said below
- partners_mid: int32 [512, 8], P(('groups', 'leaf')), parts along dimension 0, may hold values from 0 to 255, as said below
- partners_top: int32 [256, 16], P(('groups', 'leaf')), parts along dimension 0, may hold values from 0 to 127, as said below
- near_leaves: int32 [1024, 4], P(('groups', 'leaf')), parts along dimension 0, may hold values from 0 to 511, as said below
Outputs:
- product: float32 [8, 65536], P(None, ('groups', 'leaf')), parts along dimension 1
The draws below stay inside these ranges and needn't reach their ends.
There are 2 independent parts, one for each index of `groups`. The reference program is written for one: setup_inputs(seed, part) draws one part's arguments, and reference() takes and returns one part's arrays. A program takes and returns all parts, laid end to end along the dimension named above; each array names one. Nothing has to cross between parts.
Inputs may be any that keep to these rules, and one draw needn't show every extreme that they name: `partners_leaf`: in each of the four lists the nodes of one device name at most 16 entries (16 for near_leaves) held by any one device, and in every draw some device is named exactly that often by the nodes of every device. A node never names itself. `partners_mid`: as for partners_leaf, on this level. `partners_top`: as for partners_leaf, on this level. `near_leaves`: as for partners_leaf.
All inputs are finite; a program needn't handle non-finite values.
Results may differ from the reference program's by a relative error of at most 0.0063.
Values may be sent and summed in bfloat16 or wider, within the bound.
A program may use at most 64 MiB of HBM per device.

```python
import jax
import jax.numpy as jnp

LEAF = 64
RANK = 64
NV = 8
ADMIT = 4
NEAR = 4
LEAF_DEV = 32
LEAVES = 512
POINTS = 32768
NODES_MID = 256
NODES_TOP = 128
ADMIT_MID = 8
ADMIT_TOP = 16
N_LEAF = 16


def make_lists(key, nodes_dev, count):
    capacity = 2 * nodes_dev * count // N_LEAF
    hottest = jax.random.randint(jax.random.fold_in(key, 0), (), 0, N_LEAF)

    def one_device(device):
        dev_key = jax.random.fold_in(key, device + 1)
        key_order, key_place, key_within = jax.random.split(dev_key, 3)
        shuffled = jax.random.permutation(key_order, N_LEAF * capacity).astype(jnp.int32)
        elsewhere = (shuffled // capacity != hottest).astype(jnp.int32)
        arranged = shuffled[jnp.argsort(elsewhere, stable=True)]
        owners = arranged[:nodes_dev * count] // capacity
        owners = jax.random.permutation(key_place, owners).reshape(nodes_dev, count)
        position = jnp.arange(nodes_dev, dtype=jnp.int32)[:, None]
        within = jax.random.randint(key_within, (nodes_dev, count), 0, nodes_dev)
        shifted = (position + 1 + within % (nodes_dev - 1)) % nodes_dev
        within = jnp.where(owners == device, shifted, within)
        return (owners * nodes_dev + within).astype(jnp.int32)
    lists = jax.vmap(one_device)(jnp.arange(N_LEAF, dtype=jnp.int32))
    return lists.reshape(nodes_dev * N_LEAF, count)


def draw_partners_leaf(key, part):
    key = jax.random.fold_in(key, 11)
    return make_lists(key, LEAF_DEV, ADMIT)


def draw_partners_mid(key, part):
    key = jax.random.fold_in(key, 12)
    return make_lists(key, LEAF_DEV // 2, 2 * ADMIT)


def draw_partners_top(key, part):
    key = jax.random.fold_in(key, 13)
    return make_lists(key, LEAF_DEV // 4, 4 * ADMIT)


def draw_near_leaves(key, part):
    key = jax.random.fold_in(key, 14)
    return make_lists(key, LEAF_DEV, NEAR)


def levels(key, shape, cuts, smallest, high):
    gain = 1.0
    for axis_at, parts in cuts:
        heights = jax.random.uniform(jax.random.fold_in(jax.random.fold_in(key, 6), axis_at), (parts,), jnp.float32, smallest / len(cuts), high / len(cuts))
        gain = gain * jnp.repeat(jnp.exp(heights), shape[axis_at] // parts).reshape((-1,) + (1,) * (len(shape) - 1 - axis_at))
    return gain


def centred(rng, shape, spread, reach, pieces=(), kind=jnp.bfloat16):
    gain = levels(rng, shape, pieces, -0.22, 0.18) if pieces else 1.0
    drawn = jax.random.normal(rng, shape, jnp.float32) * spread * gain
    return jnp.minimum(jnp.maximum(drawn, -reach), reach).astype(kind)


def setup_inputs(seed: int = 0, part: int = 0) -> dict:
    keys = jax.random.split(jax.random.key(seed), 13)
    own_keys = jax.random.split(jax.random.fold_in(keys[12], part), 13)
    vectors = centred(own_keys[0], (NV, POINTS), 1.0, 6.0, ((1, 16),))
    leaf_bases = centred(own_keys[1], (LEAVES, LEAF * RANK), LEAF ** -0.5, 0.75, ((0, 16),))
    transfer_low = centred(own_keys[2], (LEAVES, RANK * RANK), RANK ** -0.5, 0.75, ((0, 16),))
    transfer_mid = centred(own_keys[3], (NODES_MID, RANK * RANK), RANK ** -0.5, 0.75, ((0, 16),))
    leaf_coupling_matrices = centred(own_keys[4], (LEAVES, ADMIT, RANK * RANK), (RANK * ADMIT) ** -0.5, 0.375, ((0, 16),))
    coupling_mid = centred(own_keys[5], (NODES_MID, ADMIT_MID, RANK * RANK), (RANK * ADMIT_MID) ** -0.5, 0.25, ((0, 16),))
    coupling_top = centred(own_keys[6], (NODES_TOP, ADMIT_TOP, RANK * RANK), (RANK * ADMIT_TOP) ** -0.5, 0.1875, ((0, 16),))
    near_blocks = centred(own_keys[7], (LEAVES, NEAR, LEAF * LEAF), (LEAF * NEAR) ** -0.5, 0.375, ((0, 16),))
    partners_leaf = draw_partners_leaf(jax.random.fold_in(jax.random.fold_in(keys[12], part), 71), part)
    partners_mid = draw_partners_mid(jax.random.fold_in(jax.random.fold_in(keys[12], part), 71), part)
    partners_top = draw_partners_top(jax.random.fold_in(jax.random.fold_in(keys[12], part), 71), part)
    near_leaves = draw_near_leaves(jax.random.fold_in(jax.random.fold_in(keys[12], part), 71), part)
    return dict(vectors=vectors, leaf_bases=leaf_bases, transfer_low=transfer_low, transfer_mid=transfer_mid, leaf_coupling_matrices=leaf_coupling_matrices, coupling_mid=coupling_mid, coupling_top=coupling_top, near_blocks=near_blocks, partners_leaf=partners_leaf, partners_mid=partners_mid, partners_top=partners_top, near_leaves=near_leaves)


def reference(vectors, leaf_bases, transfer_low, transfer_mid, leaf_coupling_matrices, coupling_mid, coupling_top, near_blocks, partners_leaf, partners_mid, partners_top, near_leaves):
    f32 = jnp.float32
    leaf_vecs = vectors.reshape(NV, LEAVES, LEAF).transpose(1, 0, 2)
    bases = leaf_bases.reshape(LEAVES, LEAF, RANK).astype(f32)
    up_low = transfer_low.reshape(LEAVES, RANK, RANK).astype(f32)
    up_mid = transfer_mid.reshape(NODES_MID, RANK, RANK).astype(f32)
    coefficient_leaves = jnp.einsum("nvq,nqr->nvr", leaf_vecs.astype(f32), bases).astype(jnp.bfloat16)
    coef_mid = jnp.einsum("cvs,csr->cvr", coefficient_leaves.astype(f32), up_low)
    coef_mid = coef_mid.reshape(NODES_MID, 2, NV, RANK).sum(axis=1).astype(jnp.bfloat16)
    coef_top = jnp.einsum("cvs,csr->cvr", coef_mid.astype(f32), up_mid)
    coef_top = coef_top.reshape(NODES_TOP, 2, NV, RANK).sum(axis=1).astype(jnp.bfloat16)

    def far(coef, coupling, partners):
        nodes, count = partners.shape
        selected_partners = coef[partners].astype(f32)
        matrix_stack = coupling.reshape(nodes, count, RANK, RANK).astype(f32)
        return jnp.einsum("awhz,awyz->ahy", selected_partners, matrix_stack)

    far_leaf = far(coefficient_leaves, leaf_coupling_matrices, partners_leaf)
    middle_far_field = far(coef_mid, coupling_mid, partners_mid)
    far_top = far(coef_top, coupling_top, partners_top)
    down_top = far_top.astype(jnp.bfloat16)
    parents = jnp.repeat(down_top, 2, axis=0).astype(f32)
    down_mid = (middle_far_field + jnp.einsum("cvr,csr->cvs", parents, up_mid)).astype(jnp.bfloat16)
    parents = jnp.repeat(down_mid, 2, axis=0).astype(f32)
    down_leaf = (far_leaf + jnp.einsum("cvr,csr->cvs", parents, up_low)).astype(jnp.bfloat16)
    result = jnp.einsum("nvr,nqr->nvq", down_leaf.astype(f32), bases)
    neighbours = leaf_vecs[near_leaves].astype(f32)
    blocks = near_blocks.reshape(LEAVES, NEAR, LEAF, LEAF).astype(f32)
    result = result + jnp.einsum("nkvt,nkqt->nvq", neighbours, blocks)
    return result.transpose(1, 0, 2).reshape(NV, POINTS)
```

```python
import functools

import jax
import jax.numpy as jnp
from jax import lax
from jax.experimental import pallas as pl
from jax.experimental.pallas import tpu as pltpu
from jax.sharding import PartitionSpec as P

F32 = jnp.float32
BF16 = jnp.bfloat16
VMEM = pl.BlockSpec(memory_space=pltpu.VMEM)
SMEM = pl.BlockSpec(memory_space=pltpu.SMEM)


def iota(shape, axis):
    return lax.broadcasted_iota(jnp.int32, shape, axis)


def low_half(rows):
    return iota((rows, 128), 1) < 64


def dot(a, b):
    return jnp.dot(a, b, preferred_element_type=F32)


def dot_t(a, b):
    return lax.dot_general(a, b, (((1,), (1,)), ((), ())), preferred_element_type=F32)


def spread_matrix():
    row, col = iota((128, 1024), 0), iota((128, 1024), 1)
    same = (row >> 6) == (col >> 9)
    q = 2 * ((col & 255) >> 3) + ((col >> 8) & 1)
    return jnp.where(same & ((row & 63) == q), 1.0, 0.0).astype(BF16)


def fold_matrix(count):
    row, col = iota((64 * count, 128), 0), iota((64 * count, 128), 1)
    s = 2 * ((row & (32 * count - 1)) // count) + row // (32 * count)
    return jnp.where((col & 63) == s, 1.0, 0.0).astype(BF16)


def lift(pairs, matrices, spread):
    rows = pairs.shape[0]
    wide = dot(pairs, spread)
    lane, row = iota((rows, 256), 1) & 7, (iota((rows, 256), 0) >> 3) & 3
    parts = []
    for h in range(2):
        keep = lane == 2 * row + h
        for b in range(2):
            at = (2 * h + b) * 256
            parts.append(jnp.where(keep, wide[:, at : at + 256], 0.0).astype(BF16))
    low = low_half(32)
    even, odd = [], []
    for t in range(rows // 32):
        mine = jnp.concatenate([p[32 * t : 32 * t + 32] for p in parts], axis=0)
        out = dot(mine, matrices[256 * t : 256 * t + 256, :])
        even.append(jnp.where(low, out[0:32], out[32:64]))
        odd.append(jnp.where(low, out[64:96], out[96:128]))
    return jnp.concatenate(even, axis=0), jnp.concatenate(odd, axis=0)


def both_halves(z):
    return z + pltpu.roll(z, 64, 1)


def pair_up(dup):
    rows = dup.shape[0]
    four = dup.reshape(rows // 16, 2, 8, 128)
    even = four[:, 0].reshape(rows // 2, 128)
    odd = four[:, 1].reshape(rows // 2, 128)
    return jnp.where(low_half(rows // 2), even, odd)


def upsweep(vec_ref, bases, low, mid):
    pairs = jnp.concatenate([vec_ref[:, 128 * i : 128 * i + 128].astype(F32) for i in range(16)], axis=0)
    spread = spread_matrix()
    near = pairs.astype(BF16)
    even, odd = lift(near, bases, spread)
    leaf = jnp.where(low_half(128), both_halves(even), both_halves(odd))
    even, odd = lift(leaf.astype(BF16), low, spread)
    mids = pair_up(both_halves(even + odd))
    even, odd = lift(mids.astype(BF16), mid, spread)
    tops = pair_up(both_halves(even + odd))
    return pairs, leaf, mids, tops


def up_kernel(vec_ref, bases_ref, low_ref, mid_ref, table_ref):
    parts = upsweep(vec_ref, bases_ref, low_ref, mid_ref)
    at = 0
    for part in parts:
        count = part.shape[0] // 8
        table_ref[at : at + count] = part.astype(BF16).reshape(count, 8, 128)
        at += count


def blocks_of(tile, other):
    low = low_half(8)
    return [jnp.where(low, tile, 0.0), jnp.where(low, 0.0, other)]


def gather_blocks(table_ref, node, per_dev, offset):
    shift = per_dev.bit_length() - 1
    at = (node >> shift) * 44 + offset + ((node & (per_dev - 1)) >> 1)
    tile = table_ref[at].astype(F32)
    turned = pltpu.roll(tile, 64, 1)
    first = (node & 1) == 0
    return blocks_of(jnp.where(first, tile, turned), jnp.where(first, turned, tile))


def couple_small(list_ref, table_ref, matrix_ref, per_dev, offset, out_ref):
    lane = iota((16, 128), 1) & 3

    def step(n, carry):
        rows = []
        for k in range(4):
            rows += gather_blocks(table_ref, list_ref[n, k], per_dev, offset)
        mine = jnp.concatenate(rows, axis=0).astype(BF16)
        at = pl.multiple_of(n * 128, 128)
        out = dot_t(mine, matrix_ref[pl.ds(at, 128), :])
        merged = out[0:16]
        for k in range(1, 4):
            merged = jnp.where(lane == k, out[16 * k : 16 * k + 16], merged)
        to = pl.ds(pl.multiple_of(n * 8, 8), 8)
        out_ref[to, 0:128] = merged[0:8]
        out_ref[to, 128:256] = merged[8:16]
        return carry

    lax.fori_loop(0, 32, step, 0, unroll=4)


def couple_wide(list_ref, table_ref, matrix_ref, nodes, halves, per_dev, offset, out_ref):
    lane = iota((16, 256), 1) & 7

    def step(n, carry):
        total = None
        for half in range(halves):
            rows = []
            for k in range(8):
                rows += gather_blocks(table_ref, list_ref[n, 8 * half + k], per_dev, offset)
            mine = jnp.concatenate(rows, axis=0).astype(BF16)
            at = pl.multiple_of((n * halves + half) * 256, 256)
            out = dot_t(mine, matrix_ref[pl.ds(at, 256), :])
            merged = out[0:16]
            for k in range(1, 8):
                merged = jnp.where(lane == k, out[16 * k : 16 * k + 16], merged)
            total = merged if total is None else total + merged
        to = pl.ds(pl.multiple_of(n * 8, 8), 8)
        out_ref[to, 0:256] = total[0:8]
        out_ref[to, 256:512] = total[8:16]
        return carry

    lax.fori_loop(0, nodes, step, 0, unroll=2)


def descend(parents, matrix_ref, children, shared):
    lane = iota((8, 256), 1) & 7
    outs = []
    for t in range(children // 8):
        rows = []
        for c in range(8):
            p = (8 * t + c) // shared
            d = parents[8 * p : 8 * p + 8]
            rows += blocks_of(d, d)
        mine = jnp.concatenate(rows, axis=0).astype(BF16)
        out = dot_t(mine, matrix_ref[256 * t : 256 * t + 256, :])
        for c in range(8):
            keep = lane == c
            outs.append(
                jnp.concatenate(
                    [
                        jnp.where(keep, out[16 * c : 16 * c + 8], 0.0),
                        jnp.where(keep, out[16 * c + 8 : 16 * c + 16], 0.0),
                    ],
                    axis=1,
                )
            )
    return jnp.concatenate(outs, axis=0)


def down_kernel(
    near_list, leaf_list, mid_list, top_list, table_ref,
    near_ref, leaf_ref, cmid_ref, ctop_ref, bases_ref, low_ref, mid_ref,
    out_ref, r_near, r_leaf, r_mid, r_top,
):
    couple_small(near_list, table_ref, near_ref, 32, 0, r_near)
    couple_small(leaf_list, table_ref, leaf_ref, 32, 16, r_leaf)
    couple_wide(mid_list, table_ref, cmid_ref, 16, 1, 16, 32, r_mid)
    couple_wide(top_list, table_ref, ctop_ref, 8, 2, 8, 40, r_top)
    finish(bases_ref, low_ref, mid_ref, out_ref, r_near, r_leaf, r_mid, r_top)


def finish(bases_ref, low_ref, mid_ref, out_ref, r_near, r_leaf, r_mid, r_top):
    fold4, fold8 = fold_matrix(4), fold_matrix(8)
    near_part = dot(r_near[...].astype(BF16), fold4)
    leaf_part = dot(r_leaf[...].astype(BF16), fold4)
    tops = dot(r_top[...].astype(BF16), fold8)
    mids = dot((r_mid[...] + descend(tops, mid_ref, 16, 2)).astype(BF16), fold8)
    leaves = leaf_part + dot(descend(mids, low_ref, 32, 2).astype(BF16), fold8)
    result = near_part + dot(descend(leaves, bases_ref, 32, 1).astype(BF16), fold8)
    low = low_half(8)
    for i in range(16):
        out_ref[:, 128 * i : 128 * i + 128] = jnp.where(
            low, result[16 * i : 16 * i + 8], result[16 * i + 8 : 16 * i + 16]
        )


def node_tiles(matrices):
    n = matrices.shape[0]
    return matrices.reshape(n // 8, 8, 32, 128).transpose(0, 2, 1, 3).reshape(n * 32, 128)


def list_tiles(matrices):
    n, k, _ = matrices.shape
    t = min(k, 8)
    return matrices.reshape(n, k // t, t, 32, 128).transpose(0, 1, 3, 2, 4).reshape(n * k * 32, 128)


def local(
    vectors, leaf_bases, transfer_low, transfer_mid, leaf_coupling_matrices, coupling_mid,
    coupling_top, near_blocks, partners_leaf, partners_mid, partners_top, near_leaves,
):
    bases, low, mid = node_tiles(leaf_bases), node_tiles(transfer_low), node_tiles(transfer_mid)
    table = pl.pallas_call(
        up_kernel,
        out_shape=jax.ShapeDtypeStruct((44, 8, 128), BF16),
        in_specs=[VMEM] * 4,
        out_specs=VMEM,
        compiler_params=pltpu.CompilerParams(vmem_limit_bytes=32 << 20),
    )(vectors, bases, low, mid)
    gathered = lax.all_gather(table, "leaf", axis=0, tiled=True)
    return pl.pallas_call(
        down_kernel,
        out_shape=jax.ShapeDtypeStruct(vectors.shape, F32),
        in_specs=[SMEM] * 4 + [VMEM] * 8,
        out_specs=VMEM,
        scratch_shapes=[
            pltpu.VMEM((256, 256), F32),
            pltpu.VMEM((256, 256), F32),
            pltpu.VMEM((128, 512), F32),
            pltpu.VMEM((64, 512), F32),
        ],
        compiler_params=pltpu.CompilerParams(vmem_limit_bytes=48 << 20),
    )(
        near_leaves, partners_leaf, partners_mid, partners_top, gathered,
        list_tiles(near_blocks), list_tiles(leaf_coupling_matrices), list_tiles(coupling_mid),
        list_tiles(coupling_top), bases, low, mid,
    )


def solution(mesh):
    both = ("groups", "leaf")
    in_specs = (P(None, both),) + (P(both, None),) * 3 + (P(both, None, None),) * 4 + (P(both, None),) * 4
    return jax.shard_map(local, mesh=mesh, in_specs=in_specs, out_specs=P(None, both), check_vma=False)
```

```python
import functools

import jax
import jax.numpy as jnp
from jax import lax
from jax.experimental import pallas as pl
from jax.experimental.pallas import tpu as pltpu
from jax.sharding import PartitionSpec as P

F32 = jnp.float32
BF16 = jnp.bfloat16
VMEM = pl.BlockSpec(memory_space=pltpu.VMEM)


def iota(shape, axis):
    return lax.broadcasted_iota(jnp.int32, shape, axis)


def low_half(rows):
    return iota((rows, 128), 1) < 64


def dot(a, b):
    return jnp.dot(a, b, preferred_element_type=F32)


def dot_t(a, b):
    return lax.dot_general(a, b, (((1,), (1,)), ((), ())), preferred_element_type=F32)


def spread_matrix():
    row, col = iota((128, 1024), 0), iota((128, 1024), 1)
    same = (row >> 6) == (col >> 9)
    q = 2 * ((col & 255) >> 3) + ((col >> 8) & 1)
    return jnp.where(same & ((row & 63) == q), 1.0, 0.0).astype(BF16)


def fold_matrix(count):
    row, col = iota((64 * count, 128), 0), iota((64 * count, 128), 1)
    s = 2 * ((row & (32 * count - 1)) // count) + row // (32 * count)
    return jnp.where((col & 63) == s, 1.0, 0.0).astype(BF16)


def lift(pairs, matrices, spread):
    rows = pairs.shape[0]
    wide = dot(pairs, spread)
    lane, row = iota((rows, 256), 1) & 7, (iota((rows, 256), 0) >> 3) & 3
    parts = []
    for h in range(2):
        keep = lane == 2 * row + h
        for b in range(2):
            at = (2 * h + b) * 256
            parts.append(jnp.where(keep, wide[:, at : at + 256], 0.0).astype(BF16))
    low = low_half(32)
    even, odd = [], []
    for t in range(rows // 32):
        mine = jnp.concatenate([p[32 * t : 32 * t + 32] for p in parts], axis=0)
        out = dot(mine, matrices[256 * t : 256 * t + 256, :])
        even.append(jnp.where(low, out[0:32], out[32:64]))
        odd.append(jnp.where(low, out[64:96], out[96:128]))
    return jnp.concatenate(even, axis=0), jnp.concatenate(odd, axis=0)


def both_halves(z):
    return z + pltpu.roll(z, 64, 1)


def pair_up(dup):
    rows = dup.shape[0]
    four = dup.reshape(rows // 16, 2, 8, 128)
    even = four[:, 0].reshape(rows // 2, 128)
    odd = four[:, 1].reshape(rows // 2, 128)
    return jnp.where(low_half(rows // 2), even, odd)


def upsweep(near, bases, low, mid):
    spread = spread_matrix()
    even, odd = lift(near, bases, spread)
    leaf = jnp.where(low_half(128), both_halves(even), both_halves(odd))
    even, odd = lift(leaf.astype(BF16), low, spread)
    mids = pair_up(both_halves(even + odd))
    even, odd = lift(mids.astype(BF16), mid, spread)
    tops = pair_up(both_halves(even + odd))
    return leaf, mids, tops


class Relay:
    def __init__(self, table, tiles, lines, rows, send_sem, recv_sem):
        self.table, self.tiles, self.lines, self.rows = table, tiles, lines, rows
        self.send_sem, self.recv_sem = send_sem, recv_sem
        me = lax.axis_index("leaf")
        self.me, self.a, self.b, self.c = me, me // (2 * rows), (me // 2) % rows, me % 2
        self.started = []

    def copy(self, source, way):
        target = self.me + (2 * self.rows, -2 * self.rows, -2, 2, 1 - 2 * self.c)[way]
        block = self.table.at[pl.ds(source * self.tiles, self.tiles)]
        return pltpu.make_async_remote_copy(
            src_ref=block, dst_ref=block, send_sem=self.send_sem.at[way, source],
            recv_sem=self.recv_sem.at[source], device_id={"leaf": target},
            device_id_type=pl.DeviceIdType.MESH,
        )

    def there(self, way):
        return (self.a + 1 < self.lines, self.a > 0, self.b > 0, self.b + 1 < self.rows, True)[way]

    def send(self, guard, source, ways):
        for way in ways:
            there = self.there(way)
            cond = guard if there is True else jnp.logical_and(guard, there)

            @pl.when(cond)
            def _():
                self.copy(source, way).start()

            self.started.append((cond, source, way))

    def arrive(self, guard, source, ways):
        @pl.when(guard)
        def _():
            self.copy(source, 4).wait_recv()

        self.send(guard, source, ways)

    def own(self):
        self.send(self.me >= 0, self.me, (0, 1, 2, 3, 4))

    def steps(self):
        a, b, c, lines, rows = self.a, self.b, self.c, self.lines, self.rows

        def place(x, y):
            return (x * rows + y) * 2 + c

        def line(dist):
            self.arrive(a - dist >= 0, place(a - dist, b), (0, 2, 3, 4))
            self.arrive(a + dist < lines, place(a + dist, b), (1, 2, 3, 4))

        def across(step, dist):
            for x in ([a] if dist == 0 else [a - dist, a + dist]):
                inside = jnp.logical_and(x >= 0, x < lines)
                self.arrive(jnp.logical_and(inside, b - step >= 0), place(x, b - step), (3, 4))
                self.arrive(jnp.logical_and(inside, b + step < rows), place(x, b + step), (2, 4))

        out = []
        for dist in range(1, lines):
            out.append(functools.partial(line, dist))
            out.append(functools.partial(across, 1, dist - 1))
        out.append(functools.partial(across, 1, lines - 1))
        for step in range(2, rows):
            for dist in range(lines):
                out.append(functools.partial(across, step, dist))
        out.append(self.other_core)
        return out

    def other_core(self):
        for x in range(self.lines * self.rows):
            self.copy(2 * x + 1 - self.c, 4).wait_recv()

    def finish(self):
        for cond, source, way in self.started:

            @pl.when(cond)
            def _(source=source, way=way):
                self.copy(source, way).wait_send()


def greet(relay):
    barrier = pltpu.get_barrier_semaphore()
    count = jnp.int32(1)
    for way, step in enumerate((2 * relay.rows, -2 * relay.rows, -2, 2, 1 - 2 * relay.c)):
        there = relay.there(way)
        if there is True:
            there = relay.me >= 0
        else:
            count = count + jnp.where(there, 1, 0)

        @pl.when(there)
        def _():
            pl.semaphore_signal(
                barrier, inc=1, device_id={"leaf": relay.me + step}, device_id_type=pl.DeviceIdType.MESH
            )

    pl.semaphore_wait(barrier, count)


def blocks_of(tile, other):
    low = low_half(8)
    return [jnp.where(low, tile, 0.0), jnp.where(low, 0.0, other)]


def gather_blocks(table_ref, node, per_dev, tiles, offset):
    shift = per_dev.bit_length() - 1
    at = (node >> shift) * tiles + offset + ((node & (per_dev - 1)) >> 1)
    tile = table_ref[at].astype(F32)
    turned = pltpu.roll(tile, 64, 1)
    first = (node & 1) == 0
    return blocks_of(jnp.where(first, tile, turned), jnp.where(first, turned, tile))


def couple_small(list_ref, table_ref, matrix_ref, tiles, out_ref, first=0, last=32):
    lane = iota((16, 128), 1) & 3

    def step(n, carry):
        rows = []
        for k in range(4):
            rows += gather_blocks(table_ref, list_ref[k, n], 32, tiles, 0)
        mine = jnp.concatenate(rows, axis=0).astype(BF16)
        at = pl.multiple_of(n * 128, 128)
        out = dot_t(mine, matrix_ref[pl.ds(at, 128), :])
        merged = out[0:16]
        for k in range(1, 4):
            merged = jnp.where(lane == k, out[16 * k : 16 * k + 16], merged)
        to = pl.ds(pl.multiple_of(n * 8, 8), 8)
        out_ref[to, 0:128] = merged[0:8]
        out_ref[to, 128:256] = merged[8:16]
        return carry

    lax.fori_loop(first, last, step, 0, unroll=4)


def couple_wide(list_ref, table_ref, matrix_ref, nodes, halves, per_dev, offset, flipped, out_ref):
    lane = iota((16, 256), 1) & 7

    def step(n, carry):
        total = None
        for half in range(halves):
            rows = []
            for k in range(8):
                node = list_ref[8 * half + k, n] if flipped else list_ref[n, 8 * half + k]
                rows += gather_blocks(table_ref, node, per_dev, 28, offset)
            mine = jnp.concatenate(rows, axis=0).astype(BF16)
            at = pl.multiple_of((n * halves + half) * 256, 256)
            out = dot_t(mine, matrix_ref[pl.ds(at, 256), :])
            merged = out[0:16]
            for k in range(1, 8):
                merged = jnp.where(lane == k, out[16 * k : 16 * k + 16], merged)
            total = merged if total is None else total + merged
        to = pl.ds(pl.multiple_of(n * 8, 8), 8)
        out_ref[to, 0:256] = total[0:8]
        out_ref[to, 256:512] = total[8:16]
        return carry

    lax.fori_loop(0, nodes, step, 0, unroll=2)


def descend(parents, matrix_ref, children, shared):
    lane = iota((8, 256), 1) & 7
    outs = []
    for t in range(children // 8):
        rows = []
        for c in range(8):
            p = (8 * t + c) // shared
            d = parents[8 * p : 8 * p + 8]
            rows += blocks_of(d, d)
        mine = jnp.concatenate(rows, axis=0).astype(BF16)
        out = dot_t(mine, matrix_ref[256 * t : 256 * t + 256, :])
        for c in range(8):
            keep = lane == c
            outs.append(
                jnp.concatenate(
                    [
                        jnp.where(keep, out[16 * c : 16 * c + 8], 0.0),
                        jnp.where(keep, out[16 * c + 8 : 16 * c + 16], 0.0),
                    ],
                    axis=1,
                )
            )
    return jnp.concatenate(outs, axis=0)


def kernel(lines, rows, *refs):
    vec_hbm, lists_hbm, mats_hbm, out_ref = refs[0], refs[1:5], refs[5:12], refs[12]
    lists, mats = refs[13:17], refs[17:24]
    near_table, coef_table, r_near, r_leaf, r_mid, r_top = refs[24:30]
    local_sem, near_send, near_recv, coef_send, coef_recv = refs[30:]
    near_relay = Relay(near_table, 16, lines, rows, near_send, near_recv)
    coef_relay = Relay(coef_table, 28, lines, rows, coef_send, coef_recv)
    me = near_relay.me
    mine_near, mine_coef = pl.ds(me * 16, 16), pl.ds(me * 28, 28)
    own = pltpu.make_async_copy(vec_hbm, near_table.at[mine_near], local_sem.at[11])
    own.start()
    loads = [
        pltpu.make_async_copy(src, dst, local_sem.at[i])
        for i, (src, dst) in enumerate(zip((*mats_hbm, *lists_hbm), (*mats, *lists)))
    ]
    for load in loads:
        load.start()
    bases, low, mid, near_ref, leaf_ref, cmid_ref, ctop_ref = mats
    near_list, leaf_list, mid_list, top_list = lists
    greet(near_relay)
    own.wait()
    near_relay.own()
    for load in loads[:3]:
        load.wait()
    near = near_table[mine_near].astype(F32).reshape(128, 128).astype(BF16)
    leaf, mids, tops = upsweep(near, bases, low, mid)
    coefs = jnp.concatenate([leaf, mids, tops], axis=0)
    coef_table[mine_coef] = coefs.astype(BF16).reshape(28, 8, 128)
    coef_relay.own()
    for step in near_relay.steps():
        step()
    for load in loads[3:]:
        load.wait()
    steps = coef_relay.steps()
    done = 0
    for i, step in enumerate(steps):
        if i and done < 32:
            couple_small(near_list, near_table, near_ref, 16, r_near, done, done + 8)
            done += 8
        step()
    couple_wide(top_list, coef_table, ctop_ref, 8, 2, 8, 24, False, r_top)
    couple_wide(mid_list, coef_table, cmid_ref, 16, 1, 16, 16, True, r_mid)
    couple_small(leaf_list, coef_table, leaf_ref, 28, r_leaf)
    finish(bases, low, mid, out_ref, r_near, r_leaf, r_mid, r_top)
    near_relay.finish()
    coef_relay.finish()


def finish(self):
        for cond, source, way in self.started:

            @pl.when(cond)
            def _(source=source, way=way):
                self.copy(source, way).wait_send()


def greet(relay):
    barrier = pltpu.get_barrier_semaphore()
    count = jnp.int32(1)
    for way, step in enumerate((2 * relay.rows, -2 * relay.rows, -2, 2, 1 - 2 * relay.c)):
        there = relay.there(way)
        if there is True:
            there = relay.me >= 0
        else:
            count = count + jnp.where(there, 1, 0)

        @pl.when(there)
        def _():
            pl.semaphore_signal(
                barrier, inc=1, device_id={"leaf": relay.me + step}, device_id_type=pl.DeviceIdType.MESH
            )

    pl.semaphore_wait(barrier, count)


def blocks_of(tile, other):
    low = low_half(8)
    return [jnp.where(low, tile, 0.0), jnp.where(low, 0.0, other)]


def gather_blocks(table_ref, node, per_dev, tiles, offset):
    shift = per_dev.bit_length() - 1
    at = (node >> shift) * tiles + offset + ((node & (per_dev - 1)) >> 1)
    tile = table_ref[at].astype(F32)
    turned = pltpu.roll(tile, 64, 1)
    first = (node & 1) == 0
    return blocks_of(jnp.where(first, tile, turned), jnp.where(first, turned, tile))


def couple_small(list_ref, table_ref, matrix_ref, tiles, out_ref, first=0, last=32):
    lane = iota((16, 128), 1) & 3

    def step(n, carry):
        rows = []
        for k in range(4):
            rows += gather_blocks(table_ref, list_ref[k, n], 32, tiles, 0)
        mine = jnp.concatenate(rows, axis=0).astype(BF16)
        at = pl.multiple_of(n * 128, 128)
        out = dot_t(mine, matrix_ref[pl.ds(at, 128), :])
        merged = out[0:16]
        for k in range(1, 4):
            merged = jnp.where(lane == k, out[16 * k : 16 * k + 16], merged)
        to = pl.ds(pl.multiple_of(n * 8, 8), 8)
        out_ref[to, 0:128] = merged[0:8]
        out_ref[to, 128:256] = merged[8:16]
        return carry

    lax.fori_loop(first, last, step, 0, unroll=4)


def couple_wide(list_ref, table_ref, matrix_ref, nodes, halves, per_dev, offset, flipped, out_ref):
    lane = iota((16, 256), 1) & 7

    def step(n, carry):
        total = None
        for half in range(halves):
            rows = []
            for k in range(8):
                node = list_ref[8 * half + k, n] if flipped else list_ref[n, 8 * half + k]
                rows += gather_blocks(table_ref, node, per_dev, 28, offset)
            mine = jnp.concatenate(rows, axis=0).astype(BF16)
            at = pl.multiple_of((n * halves + half) * 256, 256)
            out = dot_t(mine, matrix_ref[pl.ds(at, 256), :])
            merged = out[0:16]
            for k in range(1, 8):
                merged = jnp.where(lane == k, out[16 * k : 16 * k + 16], merged)
            total = merged if total is None else total + merged
        to = pl.ds(pl.multiple_of(n * 8, 8), 8)
        out_ref[to, 0:256] = total[0:8]
        out_ref[to, 256:512] = total[8:16]
        return carry

    lax.fori_loop(0, nodes, step, 0, unroll=2)


def descend(parents, matrix_ref, children, shared):
    lane = iota((8, 256), 1) & 7
    outs = []
    for t in range(children // 8):
        rows = []
        for c in range(8):
            p = (8 * t + c) // shared
            d = parents[8 * p : 8 * p + 8]
            rows += blocks_of(d, d)
        mine = jnp.concatenate(rows, axis=0).astype(BF16)
        out = dot_t(mine, matrix_ref[256 * t : 256 * t + 256, :])
        for c in range(8):
            keep = lane == c
            outs.append(
                jnp.concatenate(
                    [
                        jnp.where(keep, out[16 * c : 16 * c + 8], 0.0),
                        jnp.where(keep, out[16 * c + 8 : 16 * c + 16], 0.0),
                    ],
                    axis=1,
                )
            )
    return jnp.concatenate(outs, axis=0)


def down_kernel(
    near_list, leaf_list, mid_list, top_list, table_ref,
    near_ref, leaf_ref, cmid_ref, ctop_ref, bases_ref, low_ref, mid_ref,
    out_ref, r_near, r_leaf, r_mid, r_top,
):
    couple_small(near_list, table_ref, near_ref, 32, 0, r_near)
    couple_small(leaf_list, table_ref, leaf_ref, 32, 16, r_leaf)
    couple_wide(mid_list, table_ref, cmid_ref, 16, 1, 16, 32, r_mid)
    couple_wide(top_list, table_ref, ctop_ref, 8, 2, 8, 40, r_top)
    finish(bases_ref, low_ref, mid_ref, out_ref, r_near, r_leaf, r_mid, r_top)


def finish(bases_ref, low_ref, mid_ref, out_ref, r_near, r_leaf, r_mid, r_top):
    fold4, fold8 = fold_matrix(4), fold_matrix(8)
    near_part = dot(r_near[...].astype(BF16), fold4)
    leaf_part = dot(r_leaf[...].astype(BF16), fold4)
    tops = dot(r_top[...].astype(BF16), fold8)
    mids = dot((r_mid[...] + descend(tops, mid_ref, 16, 2)).astype(BF16), fold8)
    leaves = leaf_part + dot(descend(mids, low_ref, 32, 2).astype(BF16), fold8)
    result = near_part + dot(descend(leaves, bases_ref, 32, 1).astype(BF16), fold8)
    low = low_half(8)
    for i in range(16):
        out_ref[:, 128 * i : 128 * i + 128] = jnp.where(
            low, result[16 * i : 16 * i + 8], result[16 * i + 8 : 16 * i + 16]
        )


def node_tiles(matrices):
    n = matrices.shape[0]
    return matrices.reshape(n // 8, 8, 32, 128).transpose(0, 2, 1, 3).reshape(n * 32, 128)


def list_tiles(matrices):
    n, k, _ = matrices.shape
    t = min(k, 8)
    return matrices.reshape(n, k // t, t, 32, 128).transpose(0, 1, 3, 2, 4).reshape(n * k * 32, 128)


def local(
    vectors, leaf_bases, transfer_low, transfer_mid, leaf_coupling_matrices, coupling_mid,
    coupling_top, near_blocks, partners_leaf, partners_mid, partners_top, near_leaves,
):
    devices = lax.axis_size("leaf")
    rows = 1
    while 4 * rows * rows <= devices // 2:
        rows *= 2
    lines = devices // 2 // rows
    mats = (
        node_tiles(leaf_bases), node_tiles(transfer_low), node_tiles(transfer_mid), list_tiles(near_blocks),
        list_tiles(leaf_coupling_matrices), list_tiles(coupling_mid), list_tiles(coupling_top),
    )
    lists = (near_leaves.T, partners_leaf.T, partners_mid.T, partners_top)
    near = vectors.reshape(8, 16, 128).transpose(1, 0, 2)
    sems = pltpu.SemaphoreType.DMA
    return pl.pallas_call(
        functools.partial(kernel, lines, rows),
        out_shape=jax.ShapeDtypeStruct(vectors.shape, F32),
        in_specs=[pl.BlockSpec(memory_space=pltpu.HBM)] * 12,
        out_specs=VMEM,
        scratch_shapes=[pltpu.SMEM(x.shape, x.dtype) for x in lists]
        + [pltpu.VMEM(x.shape, x.dtype) for x in mats]
        + [
            pltpu.VMEM((devices * 16, 8, 128), BF16),
            pltpu.VMEM((devices * 28, 8, 128), BF16),
            pltpu.VMEM((256, 256), F32),
            pltpu.VMEM((256, 256), F32),
            pltpu.VMEM((128, 512), F32),
            pltpu.VMEM((64, 512), F32),
            sems((12,)),
            sems((5, devices)),
            sems((devices,)),
            sems((5, devices)),
            sems((devices,)),
        ],
        compiler_params=pltpu.CompilerParams(
            collective_id=0, has_side_effects=True, vmem_limit_bytes=62 << 20
        ),
        cost_estimate=pl.CostEstimate(flops=1 << 30, bytes_accessed=5 << 20, transcendentals=0),
    )(near, *lists, *mats)


def solution(mesh):
    both = ("groups", "leaf")
    in_specs = (P(None, both),) + (P(both, None),) * 3 + (P(both, None, None),) * 4 + (P(both, None),) * 4
    return jax.shard_map(local, mesh=mesh, in_specs=in_specs, out_specs=P(None, both), check_vma=False)
```

```python
import functools

import jax
import jax.numpy as jnp
from jax import lax
from jax.experimental import pallas as pl
from jax.experimental.pallas import tpu as pltpu
from jax.sharding import PartitionSpec as P

F32 = jnp.float32
BF16 = jnp.bfloat16
VMEM = pl.BlockSpec(memory_space=pltpu.VMEM)


def iota(shape, axis):
    return lax.broadcasted_iota(jnp.int32, shape, axis)


def low_half(rows):
    return iota((rows, 128), 1) < 64


def dot(a, b):
    return jnp.dot(a, b, preferred_element_type=F32)


def dot_t(a, b):
    return lax.dot_general(a, b, (((1,), (1,)), ((), ())), preferred_element_type=F32)


def spread_matrix():
    row, col = iota((128, 1024), 0), iota((128, 1024), 1)
    same = (row >> 6) == (col >> 9)
    q = 2 * ((col & 255) >> 3) + ((col >> 8) & 1)
    return jnp.where(same & ((row & 63) == q), 1.0, 0.0).astype(BF16)


def fold_matrix(count):
    row, col = iota((64 * count, 128), 0), iota((64 * count, 128), 1)
    s = 2 * ((row & (32 * count - 1)) // count) + row // (32 * count)
    return jnp.where((col & 63) == s, 1.0, 0.0).astype(BF16)


def lift(pairs, matrices, spread):
    rows = pairs.shape[0]
    wide = dot(pairs, spread)
    lane, row = iota((rows, 256), 1) & 7, (iota((rows, 256), 0) >> 3) & 3
    parts = []
    for h in range(2):
        keep = lane == 2 * row + h
        for b in range(2):
            at = (2 * h + b) * 256
            parts.append(jnp.where(keep, wide[:, at : at + 256], 0.0).astype(BF16))
    low = low_half(32)
    even, odd = [], []
    for t in range(rows // 32):
        mine = jnp.concatenate([p[32 * t : 32 * t + 32] for p in parts], axis=0)
        out = dot(mine, matrices[256 * t : 256 * t + 256, :])
        even.append(jnp.where(low, out[0:32], out[32:64]))
        odd.append(jnp.where(low, out[64:96], out[96:128]))
    return jnp.concatenate(even, axis=0), jnp.concatenate(odd, axis=0)


def both_halves(z):
    return z + pltpu.roll(z, 64, 1)


def pair_up(dup):
    rows = dup.shape[0]
    four = dup.reshape(rows // 16, 2, 8, 128)
    even = four[:, 0].reshape(rows // 2, 128)
    odd = four[:, 1].reshape(rows // 2, 128)
    return jnp.where(low_half(rows // 2), even, odd)


def upsweep(near, bases, low, mid):
    spread = spread_matrix()
    even, odd = lift(near, bases, spread)
    leaf = jnp.where(low_half(128), both_halves(even), both_halves(odd))
    even, odd = lift(leaf.astype(BF16), low, spread)
    mids = pair_up(both_halves(even + odd))
    even, odd = lift(mids.astype(BF16), mid, spread)
    tops = pair_up(both_halves(even + odd))
    return leaf, mids, tops


class Relay:
    def __init__(self, table, tiles, lines, rows, send_sem, recv_sem, direct):
        self.table, self.tiles, self.lines, self.rows = table, tiles, lines, rows
        self.send_sem, self.recv_sem, self.direct = send_sem, recv_sem, direct
        me = lax.axis_index("leaf")
        self.me, self.core = me, me ^ 1
        self.started = []

    def place(self, x, y):
        return self.me ^ (2 * (x * self.rows + y))

    def columns(self):
        return [self.place(x, 0) for x in range(1, self.lines)]

    def across(self):
        return [self.place(0, y) for y in range(1, self.rows)]

    def copy(self, source, target, slot):
        block = self.table.at[pl.ds(source * self.tiles, self.tiles)]
        return pltpu.make_async_remote_copy(
            src_ref=block, dst_ref=block, send_sem=self.send_sem.at[slot],
            recv_sem=self.recv_sem.at[source], device_id={"leaf": target},
            device_id_type=pl.DeviceIdType.MESH,
        )

    def send(self, source, target):
        copy = self.copy(source, target, len(self.started))
        copy.start()
        self.started.append(copy)

    def arrived(self, source):
        self.copy(source, self.core, 0).wait_recv()

    def straight(self):
        if self.direct:
            return [self.place(0, k) for k in range(1, self.lines * self.rows)]
        return self.columns() + self.across()

    def own(self):
        for target in self.straight() + [self.core]:
            self.send(self.me, target)

    def line(self):
        for source in self.columns():
            self.arrived(source)
            for target in ([] if self.direct else self.across()) + [self.core]:
                self.send(source, target)

    def second(self):
        for x in range(self.lines):
            for y in range(1, self.rows):
                source = self.place(x, y)
                self.arrived(source)
                self.send(source, self.core)

    def other_core(self):
        for k in range(self.lines * self.rows):
            self.arrived(self.place(0, k) ^ 1)

    def finish(self):
        for copy in self.started:
            copy.wait_send()


def greet(relay):
    barrier = pltpu.get_barrier_semaphore()
    peers = relay.straight() + [relay.core]
    for peer in peers:
        pl.semaphore_signal(barrier, inc=1, device_id={"leaf": peer}, device_id_type=pl.DeviceIdType.MESH)
    pl.semaphore_wait(barrier, len(peers))


def blocks_of(tile, other):
    low = low_half(8)
    return [jnp.where(low, tile, 0.0), jnp.where(low, 0.0, other)]


def gather_blocks(table_ref, node, per_dev, tiles, offset):
    shift = per_dev.bit_length() - 1
    at = (node >> shift) * tiles + offset + ((node & (per_dev - 1)) >> 1)
    tile = table_ref[at].astype(F32)
    turned = pltpu.roll(tile, 64, 1)
    first = (node & 1) == 0
    return blocks_of(jnp.where(first, tile, turned), jnp.where(first, turned, tile))


def couple_small(list_ref, table_ref, matrix_ref, tiles, out_ref, first=0, last=32):
    lane = iota((16, 128), 1) & 3

    def step(n, carry):
        rows = []
        for k in range(4):
            rows += gather_blocks(table_ref, list_ref[k, n], 32, tiles, 0)
        mine = jnp.concatenate(rows, axis=0).astype(BF16)
        at = pl.multiple_of(n * 128, 128)
        out = dot_t(mine, matrix_ref[pl.ds(at, 128), :])
        merged = out[0:16]
        for k in range(1, 4):
            merged = jnp.where(lane == k, out[16 * k : 16 * k + 16], merged)
        to = pl.ds(pl.multiple_of(n * 8, 8), 8)
        out_ref[to, 0:128] = merged[0:8]
        out_ref[to, 128:256] = merged[8:16]
        return carry

    lax.fori_loop(first, last, step, 0, unroll=8)


def couple_wide(list_ref, table_ref, matrix_ref, nodes, halves, per_dev, offset, flipped, out_ref):
    lane = iota((16, 256), 1) & 7

    def step(n, carry):
        total = None
        for half in range(halves):
            rows = []
            for k in range(8):
                node = list_ref[8 * half + k, n] if flipped else list_ref[n, 8 * half + k]
                rows += gather_blocks(table_ref, node, per_dev, 28, offset)
            mine = jnp.concatenate(rows, axis=0).astype(BF16)
            at = pl.multiple_of((n * halves + half) * 256, 256)
            out = dot_t(mine, matrix_ref[pl.ds(at, 256), :])
            merged = out[0:16]
            for k in range(1, 8):
                merged = jnp.where(lane == k, out[16 * k : 16 * k + 16], merged)
            total = merged if total is None else total + merged
        to = pl.ds(pl.multiple_of(n * 8, 8), 8)
        out_ref[to, 0:256] = total[0:8]
        out_ref[to, 256:512] = total[8:16]
        return carry

    lax.fori_loop(0, nodes, step, 0, unroll=4)


def descend(parents, matrix_ref, children, shared):
    lane = iota((8, 256), 1) & 7
    outs = []
    for t in range(children // 8):
        rows = []
        for c in range(8):
            p = (8 * t + c) // shared
            d = parents[8 * p : 8 * p + 8]
            rows += blocks_of(d, d)
        mine = jnp.concatenate(rows, axis=0).astype(BF16)
        out = dot_t(mine, matrix_ref[256 * t : 256 * t + 256, :])
        for c in range(8):
            keep = lane == c
            outs.append(
                jnp.concatenate(
                    [
                        jnp.where(keep, out[16 * c : 16 * c + 8], 0.0),
                        jnp.where(keep, out[16 * c + 8 : 16 * c + 16], 0.0),
                    ],
                    axis=1,
                )
            )
    return jnp.concatenate(outs, axis=0)


def kernel(lines, rows, *refs):
    vec_hbm, lists_hbm, mats_hbm, out_ref = refs[0], refs[1:5], refs[5:12], refs[12]
    lists, mats = refs[13:17], refs[17:24]
    near_table, coef_table, r_near, r_leaf, r_mid, r_top = refs[24:30]
    local_sem, near_send, near_recv, coef_send, coef_recv = refs[30:]
    near_relay = Relay(near_table, 16, lines, rows, near_send, near_recv, True)
    coef_relay = Relay(coef_table, 28, lines, rows, coef_send, coef_recv, False)
    me = near_relay.me
    mine_near, mine_coef = pl.ds(me * 16, 16), pl.ds(me * 28, 28)
    own = pltpu.make_async_copy(vec_hbm, near_table.at[mine_near], local_sem.at[11])
    own.start()
    loads = [
        pltpu.make_async_copy(src, dst, local_sem.at[i])
        for i, (src, dst) in enumerate(zip((*mats_hbm, *lists_hbm), (*mats, *lists)))
    ]
    for load in loads:
        load.start()
    bases, low, mid, near_ref, leaf_ref, cmid_ref, ctop_ref = mats
    near_list, leaf_list, mid_list, top_list = lists
    greet(near_relay)
    own.wait()
    near_relay.own()
    for load in loads[:3]:
        load.wait()
    near = near_table[mine_near].astype(F32).reshape(128, 128).astype(BF16)
    leaf, mids, tops = upsweep(near, bases, low, mid)
    coefs = jnp.concatenate([leaf, mids, tops], axis=0)
    coef_table[mine_coef] = coefs.astype(BF16).reshape(28, 8, 128)
    coef_relay.own()
    near_relay.line()
    near_relay.second()
    coef_relay.line()
    near_relay.other_core()
    for load in loads[3:]:
        load.wait()
    couple_small(near_list, near_table, near_ref, 16, r_near, 0, 16)
    coef_relay.second()
    couple_small(near_list, near_table, near_ref, 16, r_near, 16, 32)
    coef_relay.other_core()
    couple_wide(top_list, coef_table, ctop_ref, 8, 2, 8, 24, False, r_top)
    couple_wide(mid_list, coef_table, cmid_ref, 16, 1, 16, 16, True, r_mid)
    couple_small(leaf_list, coef_table, leaf_ref, 28, r_leaf)
    finish(bases, low, mid, out_ref, r_near, r_leaf, r_mid, r_top)
    near_relay.finish()
    coef_relay.finish()


def finish(bases_ref, low_ref, mid_ref, out_ref, r_near, r_leaf, r_mid, r_top):
    fold4, fold8 = fold_matrix(4), fold_matrix(8)
    near_part = dot(r_near[...].astype(BF16), fold4)
    leaf_part = dot(r_leaf[...].astype(BF16), fold4)
    tops = dot(r_top[...].astype(BF16), fold8)
    mids = dot((r_mid[...] + descend(tops, mid_ref, 16, 2)).astype(BF16), fold8)
    leaves = leaf_part + dot(descend(mids, low_ref, 32, 2).astype(BF16), fold8)
    result = near_part + dot(descend(leaves, bases_ref, 32, 1).astype(BF16), fold8)
    low = low_half(8)
    for i in range(16):
        out_ref[:, 128 * i : 128 * i + 128] = jnp.where(
            low, result[16 * i : 16 * i + 8], result[16 * i + 8 : 16 * i + 16]
        )


def node_tiles(matrices):
    n = matrices.shape[0]
    return matrices.reshape(n // 8, 8, 32, 128).transpose(0, 2, 1, 3).reshape(n * 32, 128)


def list_tiles(matrices):
    n, k, _ = matrices.shape
    t = min(k, 8)
    return matrices.reshape(n, k // t, t, 32, 128).transpose(0, 1, 3, 2, 4).reshape(n * k * 32, 128)


def local(
    vectors, leaf_bases, transfer_low, transfer_mid, leaf_coupling_matrices, coupling_mid,
    coupling_top, near_blocks, partners_leaf, partners_mid, partners_top, near_leaves,
):
    devices = lax.axis_size("leaf")
    rows = 1
    while 4 * rows * rows <= devices // 2:
        rows *= 2
    lines = devices // 2 // rows
    mats = (
        node_tiles(leaf_bases), node_tiles(transfer_low), node_tiles(transfer_mid), list_tiles(near_blocks),
        list_tiles(leaf_coupling_matrices), list_tiles(coupling_mid), list_tiles(coupling_top),
    )
    lists = (near_leaves.T, partners_leaf.T, partners_mid.T, partners_top)
    near = vectors.reshape(8, 16, 128).transpose(1, 0, 2)
    sems = pltpu.SemaphoreType.DMA
    return pl.pallas_call(
        functools.partial(kernel, lines, rows),
        out_shape=jax.ShapeDtypeStruct(vectors.shape, F32),
        in_specs=[pl.BlockSpec(memory_space=pltpu.HBM)] * 12,
        out_specs=VMEM,
        scratch_shapes=[pltpu.SMEM(x.shape, x.dtype) for x in lists]
        + [pltpu.VMEM(x.shape, x.dtype) for x in mats]
        + [
            pltpu.VMEM((devices * 16, 8, 128), BF16),
            pltpu.VMEM((devices * 28, 8, 128), BF16),
            pltpu.VMEM((256, 256), F32),
            pltpu.VMEM((256, 256), F32),
            pltpu.VMEM((128, 512), F32),
            pltpu.VMEM((64, 512), F32),
            sems((12,)),
            sems((devices,)),
            sems((devices,)),
            sems((devices,)),
            sems((devices,)),
        ],
        compiler_params=pltpu.CompilerParams(
            collective_id=0, has_side_effects=True, vmem_limit_bytes=62 << 20
        ),
        cost_estimate=pl.CostEstimate(flops=1 << 30, bytes_accessed=5 << 20, transcendentals=0),
    )(near, *lists, *mats)


def solution(mesh):
    both = ("groups", "leaf")
    in_specs = (P(None, both),) + (P(both, None),) * 3 + (P(both, None, None),) * 4 + (P(both, None),) * 4
    return jax.shard_map(local, mesh=mesh, in_specs=in_specs, out_specs=P(None, both), check_vma=False)
```
